32 devices in a mesh: groups: 2 (over x), seq: 16 (over z, y, core).
Axes of the slice: x: 2, y: 2, z: 4, core: 2. Of those that a mesh axis runs over, the one named last changes fastest.
Arguments:
- query: bfloat16 [8192, 1536], P(('groups', 'seq')), parts along dimension 0, may hold values from -6 to 6
- keys: bfloat16 [8192, 1536], P(('groups', 'seq')), parts along dimension 0, may hold values from -6 to 6
- values: bfloat16 [8192, 1536], P(('groups', 'seq')), parts along dimension 0, may hold values from -6 to 6
- allowed: int32 [64, 4], P(('groups', 'seq')), parts along dimension 0, may hold values from -1 to 31, as said below
- kernel: float32 [31, 1536], replicated, may hold values from -4 to 4
- cotangent: bfloat16 [8192, 1536], P(('groups', 'seq')), parts along dimension 0, may hold values from -6 to 6
Outputs:
- conv_out: bfloat16 [8192, 1536], P(('groups', 'seq')), parts along dimension 0
- query_grad: bfloat16 [8192, 1536], P(('groups', 'seq')), parts along dimension 0
- keys_grad: bfloat16 [8192, 1536], P(('groups', 'seq')), parts along dimension 0
- values_grad: bfloat16 [8192, 1536], P(('groups', 'seq')), parts along dimension 0
- kernel_grad: float32 [62, 1536], P('groups'), parts along dimension 0
The draws below stay inside these ranges and needn't reach their ends.
There are 2 independent parts, one for each index of `groups`. The reference program is written for one: setup_inputs(seed, part) draws one part's arguments, and reference() takes and returns one part's arrays. A program takes and returns all parts, laid end to end along the dimension named above; an argument that names none is the same for every part. Nothing has to cross between parts.
Inputs may be any that keep to these rules, and one draw needn't show every extreme that they name: `allowed`: row b lists b first, then three distinct earlier blocks between b - 8 and b - 1, or -1 where such a block would lie before frame 0; the last row reaches back exactly 8 blocks.
All inputs are finite; a program needn't handle non-finite values.
Results may differ from the reference program's by a relative error of at most 0.012.
Values may be sent and summed in bfloat16 or wider, within the bound.
A program may use at most 128 MiB of HBM per device.

```python
import jax
import jax.numpy as jnp
from jax import lax

D = 1536
HEADS = 24
HD = 64
KERNEL = 31
BLOCK = 128
LOOK = 4
SPAN_DEV = 4
FR_DEV = 256
FRAMES = 4096
QBLOCKS = 32


def draw_query(key, part):
    drawn = jnp.clip(jax.random.normal(jax.random.fold_in(key, 11), (FRAMES, D), jnp.float32), -6.0, 6.0)
    return drawn.astype(jnp.bfloat16)


def draw_keys(key, part):
    drawn = jnp.clip(jax.random.normal(jax.random.fold_in(key, 13), (FRAMES, D), jnp.float32), -6.0, 6.0)
    return drawn.astype(jnp.bfloat16)


def draw_allowed(key, part):
    reach = SPAN_DEV * (FR_DEV // BLOCK)
    rows = jnp.arange(QBLOCKS, dtype=jnp.int32)
    columns = jnp.arange(reach, dtype=jnp.int32)
    bits = jax.random.randint(key, (QBLOCKS, reach), 0, 1 << 20)
    ranking = bits * 64 + columns[None, :]
    forced = (rows[:, None] == QBLOCKS - 1) & (columns[None, :] == reach - 1)
    ranking = jnp.where(forced, jnp.int32(1 << 27), ranking)
    _, picked = lax.top_k(ranking, LOOK - 1)
    earlier = rows[:, None] - (picked + 1)
    earlier = jnp.where(earlier < 0, -1, earlier)
    return jnp.concatenate([rows[:, None], earlier], axis=1).astype(jnp.int32)


def block_levels(stream_key, extent, cuts, least, high):
    loudness, own = 1.0, jax.random.fold_in(stream_key, 6)
    for position, parts in cuts:
        draws = jnp.exp(jax.random.uniform(jax.random.fold_in(own, position), (parts,), jnp.float32, least / len(cuts), high / len(cuts)))
        loudness = loudness * jnp.repeat(draws, extent[position] // parts).reshape([-1 if axis == position else 1 for axis in range(len(extent))])
    return loudness


def scatter_about(rng, shape, scale, most, split=(), held_as=jnp.bfloat16):
    gain = block_levels(rng, shape, split, -0.22, 0.18) if split else 1.0
    values = jax.random.normal(rng, shape, jnp.float32) * scale * gain
    return jnp.minimum(jnp.maximum(values, -most), most).astype(held_as)


def setup_inputs(seed: int = 0, part: int = 0) -> dict:
    key_list = jax.random.split(jax.random.key(seed), 7)
    own_keys = jax.random.split(jax.random.fold_in(key_list[6], part), 7)
    query = draw_query(jax.random.fold_in(jax.random.fold_in(key_list[6], part), 71), part)
    keys = draw_keys(jax.random.fold_in(jax.random.fold_in(key_list[6], part), 71), part)
    values = scatter_about(own_keys[2], (FRAMES, D), 1.0, 6.0, ((0, 16),))
    allowed = draw_allowed(jax.random.fold_in(jax.random.fold_in(key_list[6], part), 71), part)
    kernel = scatter_about(key_list[4], (KERNEL, D), 1.0, 4.0, (), jnp.float32)
    cotangent = scatter_about(own_keys[5], (FRAMES, D), 1.0, 6.0, ((0, 16),))
    return {"query": query, "keys": keys, "values": values, "allowed": allowed, "kernel": kernel, "cotangent": cotangent}


SCALE = 0.125
NEG = -1e30


def split_heads(matrix):
    return matrix.reshape(matrix.shape[0], HEADS, HD).transpose(1, 0, 2)


def join_heads(array):
    return array.transpose(1, 0, 2).reshape(array.shape[1], HEADS * HD)


def gather_blocks(matrix, block_ids):
    safe_ids = jnp.maximum(block_ids, 0).astype(jnp.int32)
    pieces = [lax.dynamic_slice_in_dim(matrix, safe_ids[column] * BLOCK, BLOCK, 0) for column in range(LOOK)]
    return jnp.concatenate(pieces, axis=0)


def block_probs(query_block, key_block, valid):
    scores = jnp.einsum("hqd,hkd->hqk", query_block.astype(jnp.float32), key_block.astype(jnp.float32)) * SCALE
    scores = jnp.where(valid[None, None, :], scores, NEG)
    peak = jnp.max(scores, axis=-1, keepdims=True)
    expo = jnp.exp(scores - peak)
    return expo / jnp.sum(expo, axis=-1, keepdims=True)


def reference(query, keys, values, allowed, kernel, cotangent):
    half = KERNEL // 2

    def pieces_of(block):
        block_ids = allowed[block]
        query_block = split_heads(lax.dynamic_slice_in_dim(query, block * BLOCK, BLOCK, 0))
        key_block = split_heads(gather_blocks(keys, block_ids))
        value_block = split_heads(gather_blocks(values, block_ids))
        valid = jnp.repeat(block_ids >= 0, BLOCK)
        return block_ids, query_block, key_block, value_block, valid

    def forward_block(block):
        block_ids, query_block, key_block, value_block, valid = pieces_of(block)
        probs = block_probs(query_block, key_block, valid)
        probs_half = lax.optimization_barrier(probs.astype(jnp.bfloat16)).astype(jnp.float32)
        attended = jnp.einsum("hqk,hkd->hqd", probs_half, value_block.astype(jnp.float32))
        return join_heads(attended)

    blocks = jnp.arange(QBLOCKS, dtype=jnp.int32)
    attended = lax.map(forward_block, blocks).reshape(FRAMES, D)
    attended_half = attended.astype(jnp.bfloat16)
    padded = jnp.pad(attended_half, ((half, half), (0, 0))).astype(jnp.float32)
    cot_pad = jnp.pad(cotangent, ((half, half), (0, 0))).astype(jnp.float32)
    conv_sum = jnp.zeros((FRAMES, D), jnp.float32)
    grad_sum = jnp.zeros((FRAMES, D), jnp.float32)
    taps_grad = []
    cot_float = cotangent.astype(jnp.float32)
    for offset in range(KERNEL):
        conv_sum = conv_sum + kernel[offset][None, :] * padded[offset:offset + FRAMES]
        grad_sum = grad_sum + kernel[offset][None, :] * cot_pad[2 * half - offset:2 * half - offset + FRAMES]
        taps_grad.append(jnp.sum(cot_float * padded[offset:offset + FRAMES], axis=0))
    conv_out = conv_sum.astype(jnp.bfloat16)
    attended_grad = grad_sum.astype(jnp.bfloat16)
    kernel_grad = jnp.stack(taps_grad)

    def backward_block(carry, block):
        keys_acc, values_acc = carry
        block_ids, query_block, key_block, value_block, valid = pieces_of(block)
        probs = block_probs(query_block, key_block, valid)
        probs_half = lax.optimization_barrier(probs.astype(jnp.bfloat16)).astype(jnp.float32)
        grad_block = split_heads(lax.dynamic_slice_in_dim(attended_grad, block * BLOCK, BLOCK, 0)).astype(jnp.float32)
        out_block = split_heads(lax.dynamic_slice_in_dim(attended, block * BLOCK, BLOCK, 0))
        probs_grad = jnp.einsum("hqd,hkd->hqk", grad_block, value_block.astype(jnp.float32))
        delta = jnp.sum(grad_block * out_block, axis=-1, keepdims=True)
        scores_grad = (SCALE * probs * (probs_grad - delta)).astype(jnp.bfloat16)
        scores_grad = lax.optimization_barrier(scores_grad).astype(jnp.float32)
        query_part = jnp.einsum("hqk,hkd->hqd", scores_grad, key_block.astype(jnp.float32))
        keys_part = join_heads(jnp.einsum("hqk,hqd->hkd", scores_grad, query_block.astype(jnp.float32)))
        values_part = join_heads(jnp.einsum("hqk,hqd->hkd", probs_half, grad_block))
        safe_ids = jnp.maximum(block_ids, 0).astype(jnp.int32)
        for column in range(LOOK):
            start = safe_ids[column] * BLOCK
            rows_k = lax.dynamic_slice_in_dim(keys_acc, start, BLOCK, 0)
            rows_v = lax.dynamic_slice_in_dim(values_acc, start, BLOCK, 0)
            keys_acc = lax.dynamic_update_slice_in_dim(keys_acc, rows_k + keys_part[column * BLOCK:(column + 1) * BLOCK], start, 0)
            values_acc = lax.dynamic_update_slice_in_dim(values_acc, rows_v + values_part[column * BLOCK:(column + 1) * BLOCK], start, 0)
        return (keys_acc, values_acc), join_heads(query_part).astype(jnp.bfloat16)

    start_acc = (jnp.zeros((FRAMES, D), jnp.float32), jnp.zeros((FRAMES, D), jnp.float32))
    (keys_acc, values_acc), query_rows = lax.scan(backward_block, start_acc, blocks)
    query_grad = query_rows.reshape(FRAMES, D)
    return (conv_out, query_grad, keys_acc.astype(jnp.bfloat16), values_acc.astype(jnp.bfloat16), kernel_grad)
```

```python
import functools

import jax
import jax.numpy as jnp
from jax import lax
from jax.experimental import pallas as pl
from jax.experimental.pallas import tpu as pltpu
from jax.sharding import PartitionSpec as P

HD = 64
KERNEL = 31
HALF = KERNEL // 2
BLOCK = 128
LOOK = 4
SPAN_DEV = 4
LANES = 128
HALO = 16
ROWS = 64
CHUNKS = 3

SCALE = 0.125
NEG = -1e30
NT = (((1,), (1,)), ((), ()))
TN = (((0,), (0,)), ((), ()))
NN = (((1,), (0,)), ((), ()))


def dot(a, b, dims):
    return lax.dot_general(a, b, dims, preferred_element_type=jnp.float32)


def fill(pad, low_ref, mid_ref, high_ref):
    frames = mid_ref.shape[0]
    pad[0:HALO] = low_ref[...].astype(jnp.float32)
    pad[HALO:HALO + frames] = mid_ref[...].astype(jnp.float32)
    pad[HALO + frames:2 * HALO + frames] = high_ref[...].astype(jnp.float32)


def conv_kernel(flip, taps_ref, low_ref, mid_ref, high_ref, out_ref, pad):
    frames = mid_ref.shape[0]
    fill(pad, low_ref, mid_ref, high_ref)
    for base in range(0, frames, ROWS):
        total = jnp.zeros((ROWS, LANES), jnp.float32)
        for tap in range(KERNEL):
            reach = HALF - tap if flip else tap - HALF
            start = base + HALO + reach
            total += taps_ref[tap:tap + 1, :] * pad[start:start + ROWS, :]
        out_ref[base:base + ROWS, :] = total.astype(out_ref.dtype)


def taps_kernel(low_ref, mid_ref, high_ref, att_ref, out_ref, pad):
    frames = mid_ref.shape[0]
    fill(pad, low_ref, mid_ref, high_ref)
    for base in range(0, frames, ROWS):
        att = att_ref[base:base + ROWS, :].astype(jnp.float32)
        for tap in range(KERNEL):
            start = base + HALO + HALF - tap
            part = jnp.sum(att * pad[start:start + ROWS, :], axis=0, keepdims=True)
            if base == 0:
                out_ref[tap:tap + 1, :] = part
            else:
                out_ref[tap:tap + 1, :] += part


def column_specs(rows):
    return [pl.BlockSpec((r, LANES), lambda i: (0, i)) for r in rows]


def conv(flip, taps, low, mid, high):
    frames, width = mid.shape
    return pl.pallas_call(
        functools.partial(conv_kernel, flip),
        grid=(width // LANES,),
        in_specs=column_specs((KERNEL, HALO, frames, HALO)),
        out_specs=column_specs((frames,))[0],
        out_shape=jax.ShapeDtypeStruct((frames, width), jnp.bfloat16),
        scratch_shapes=[pltpu.VMEM((frames + 2 * HALO, LANES), jnp.float32)],
        cost_estimate=pl.CostEstimate(
            flops=2 * KERNEL * frames * width, bytes_accessed=16 * frames * width, transcendentals=0
        ),
    )(taps, low, mid, high)


def taps_sum(low, mid, high, att):
    frames, width = mid.shape
    return pl.pallas_call(
        taps_kernel,
        grid=(width // LANES,),
        in_specs=column_specs((HALO, frames, HALO, frames)),
        out_specs=column_specs((KERNEL,))[0],
        out_shape=jax.ShapeDtypeStruct((KERNEL, width), jnp.float32),
        scratch_shapes=[pltpu.VMEM((frames + 2 * HALO, LANES), jnp.float32)],
        cost_estimate=pl.CostEstimate(
            flops=2 * KERNEL * frames * width, bytes_accessed=16 * frames * width, transcendentals=0
        ),
    )(low, mid, high, att)


def attention_kernel(first, slots, bias, q_ref, g_ref, k_ref, v_ref, b_ref, m_ref, y_ref, d_ref, *rest):
    if not first:
        rest = rest[2:]
    att_ref, dq_ref, ga_ref, gb_ref, gm_ref, gy_ref, gd_ref, kc, vc, dkc, dvc = rest
    frames = q_ref.shape[0]
    held = frames // BLOCK
    own = (held, BLOCK, LANES)
    kc[0:held] = k_ref[...].reshape(own)
    vc[0:held] = v_ref[...].reshape(own)
    for place, ref in enumerate((b_ref, m_ref, y_ref, d_ref)):
        at = held * (place + 1)
        kc[at:at + held] = ref[0].reshape(own)
        vc[at:at + held] = ref[1].reshape(own)
    dkc[...] = jnp.zeros_like(dkc)
    dvc[...] = jnp.zeros_like(dvc)
    low_head = lax.broadcasted_iota(jnp.int32, (BLOCK, LANES), 1) < HD

    def both(rows):
        zero = jnp.zeros_like(rows)
        return jnp.concatenate([jnp.where(low_head, rows, zero), jnp.where(low_head, zero, rows)], axis=0)

    for block in range(held):
        rows = slice(block * BLOCK, (block + 1) * BLOCK)
        query = both(q_ref[rows, :] * SCALE)
        grad = both(g_ref[rows, :])
        spots = [slots[block, j] for j in range(LOOK)]
        kk = jnp.concatenate([kc[s] for s in spots], axis=0)
        vv = jnp.concatenate([vc[s] for s in spots], axis=0)
        scores = dot(kk, query, NT)
        scores = jnp.concatenate(
            [scores[j * BLOCK:(j + 1) * BLOCK] + bias[block, j] for j in range(LOOK)], axis=0
        )
        peak = jnp.max(scores, axis=0, keepdims=True)
        expo = jnp.exp(scores - peak)
        probs = expo * (1.0 / jnp.sum(expo, axis=0, keepdims=True))
        probs_half = probs.astype(jnp.bfloat16)
        out = dot(probs_half, vv, TN)
        att_ref[rows, :] = jnp.where(low_head, out[:BLOCK], out[BLOCK:]).astype(att_ref.dtype)
        probs_grad = dot(vv, grad, NT)
        delta = jnp.sum(probs_half.astype(jnp.float32) * probs_grad, axis=0, keepdims=True)
        scores_grad = (probs * (probs_grad - delta)).astype(jnp.bfloat16)
        back = dot(scores_grad, kk, TN)
        dq_ref[rows, :] = (SCALE * jnp.where(low_head, back[:BLOCK], back[BLOCK:])).astype(dq_ref.dtype)
        dk = dot(scores_grad, query, NN)
        dv = dot(probs_half, grad, NN)
        for j in range(LOOK):
            dkc[spots[j]] += dk[j * BLOCK:(j + 1) * BLOCK]
            dvc[spots[j]] += dv[j * BLOCK:(j + 1) * BLOCK]
    for place, ref in enumerate((ga_ref, gb_ref, gm_ref, gy_ref, gd_ref)):
        at = held * place
        ref[0] = dkc[at:at + held].reshape(frames, LANES).astype(ref.dtype)
        ref[1] = dvc[at:at + held].reshape(frames, LANES).astype(ref.dtype)


def attention(chunk, slots, bias, query, grad, keys, values, pieces, carried):
    frames, width = query.shape
    part = width // CHUNKS
    steps = part // LANES
    base = chunk * steps
    held = frames // BLOCK
    wide = pl.BlockSpec((frames, LANES), lambda i: (0, base + i))
    piece = pl.BlockSpec((2, frames, LANES), lambda i: (0, 0, i))
    smem = pl.BlockSpec(memory_space=pltpu.SMEM)
    whole = jax.ShapeDtypeStruct((frames, width), jnp.bfloat16)
    term = jax.ShapeDtypeStruct((2, frames, part), jnp.bfloat16)
    count = held * (SPAN_DEV + 1)
    return pl.pallas_call(
        functools.partial(attention_kernel, not carried),
        grid=(steps,),
        in_specs=[smem, smem] + [wide] * 4 + [piece] * 4 + [pl.BlockSpec(memory_space=pl.ANY)] * len(carried),
        out_specs=[wide] * 2 + [piece] * 5,
        out_shape=[whole] * 2 + [term] * 5,
        scratch_shapes=[
            pltpu.VMEM((count, BLOCK, LANES), jnp.bfloat16),
            pltpu.VMEM((count, BLOCK, LANES), jnp.bfloat16),
            pltpu.VMEM((count, BLOCK, LANES), jnp.float32),
            pltpu.VMEM((count, BLOCK, LANES), jnp.float32),
        ],
        input_output_aliases={10: 0, 11: 1} if carried else {},
        compiler_params=pltpu.CompilerParams(vmem_limit_bytes=32 * 1024 * 1024),
        cost_estimate=pl.CostEstimate(
            flops=12 * LOOK * BLOCK * frames * part * 4,
            bytes_accessed=30 * frames * part,
            transcendentals=LOOK * BLOCK * frames * part // HD,
        ),
    )(slots, bias, query, grad, keys, values, *pieces, *carried)


def local(query, keys, values, allowed, kernel, cotangent):
    frames, width = query.shape
    held = frames // BLOCK
    count = lax.axis_size("seq")
    own = lax.axis_index("seq")
    odd_core = (own % 2) == 1
    odd_pair = ((own // 2) % 2) == 1
    part = width // CHUNKS
    up = [(i, i + SPAN_DEV) for i in range(count - SPAN_DEV)]
    down = [(b, a) for a, b in up]
    mate = [(i, i ^ 1) for i in range(count)]
    across = [(i, i ^ 2) for i in range(count)]
    forward = [(i, i + 1) for i in range(count - 1)]
    backward = [(b, a) for a, b in forward]

    def halo(rows):
        return (
            lax.ppermute(rows[frames - HALO:], "seq", forward),
            lax.ppermute(rows[:HALO], "seq", backward),
        )

    cot_low, cot_high = halo(cotangent)
    distance = jnp.clip(own - jnp.maximum(allowed, 0) // held, 0, SPAN_DEV)
    table = jnp.where(odd_core, jnp.array([0, 2, 3, 4, 1]), jnp.array([0, 4, 3, 2, 1]))
    valid = allowed >= 0
    slots = jnp.where(valid, table[distance] * held + allowed % held, 0).astype(jnp.int32)
    bias = jnp.where(valid, 0.0, NEG).astype(jnp.float32)

    received = []
    for chunk in range(CHUNKS):
        columns = slice(chunk * part, (chunk + 1) * part)
        here = jnp.stack([keys[:, columns], values[:, columns]])
        behind = lax.ppermute(here, "seq", up)
        beside = lax.ppermute(jnp.where(odd_pair, behind, here), "seq", across)
        near = lax.ppermute(jnp.where(odd_core, behind, here), "seq", mate)
        far = lax.ppermute(beside, "seq", mate)
        received.append((behind, near, beside, far))

    attended_grad = conv(True, kernel, cot_low, cotangent, cot_high)
    carried = ()
    terms = []
    for chunk in range(CHUNKS):
        done = attention(
            chunk, slots, bias, query, attended_grad, keys, values, received[chunk], carried
        )
        carried = tuple(done[:2])
        terms.append(done[2:])
    attended, query_grad = carried

    def masked(flag, array):
        return jnp.where(flag, array.astype(jnp.float32), 0.0)

    sums = []
    for here, behind, near, beside, far in terms:
        near_in = lax.ppermute(near, "seq", mate)
        far_in = lax.ppermute(far, "seq", mate)
        wide = beside.astype(jnp.float32) + far_in.astype(jnp.float32)
        beside_in = lax.ppermute(wide.astype(jnp.bfloat16), "seq", across)
        back = behind.astype(jnp.float32) + masked(odd_core, near_in) + masked(odd_pair, beside_in)
        behind_in = lax.ppermute(back.astype(jnp.bfloat16), "seq", down)
        total = here.astype(jnp.float32) + masked(~odd_core, near_in) + masked(~odd_pair, beside_in)
        sums.append((total + behind_in.astype(jnp.float32)).astype(jnp.bfloat16))
    att_low, att_high = halo(attended)
    kernel_grad = lax.psum(taps_sum(cot_low, cotangent, cot_high, attended), "seq")
    conv_out = conv(False, kernel, att_low, attended, att_high)
    keys_grad = jnp.concatenate([s[0] for s in sums], axis=1)
    values_grad = jnp.concatenate([s[1] for s in sums], axis=1)
    return (conv_out, query_grad, keys_grad, values_grad, kernel_grad)


def solution(mesh):
    rows = P(("groups", "seq"), None)
    return jax.shard_map(
        local,
        mesh=mesh,
        in_specs=(rows, rows, rows, rows, P(), rows),
        out_specs=(rows, rows, rows, rows, P("groups", None)),
        check_vma=False,
    )
```

```python
import functools

import jax
import jax.numpy as jnp
from jax import lax
from jax.experimental import pallas as pl
from jax.experimental.pallas import tpu as pltpu
from jax.sharding import PartitionSpec as P

HD = 64
KERNEL = 31
HALF = KERNEL // 2
TAPS = 32
BLOCK = 128
LOOK = 4
SPAN_DEV = 4
LANES = 128
HALO = 16
ROWS = 64
AHEAD = 2

SCALE = 0.125
NEG = -1e30
NT = (((1,), (1,)), ((), ()))
TN = (((0,), (0,)), ((), ()))
NN = (((1,), (0,)), ((), ()))
MESH = pl.DeviceIdType.MESH
Z, Y, M, D, BM, BD, BY, BZ = range(8)


def dot(a, b, dims):
    return lax.dot_general(a, b, dims, preferred_element_type=jnp.float32)


def whole_kernel(
    count, slots, back, bias, q_ref, k_hbm, v_hbm, taps_ref, cot_ref,
    conv_ref, dq_ref, dk_ref, dv_ref, kg_ref,
    own, behind, near, beside, far,
    g_own, g_behind, g_near, g_beside, g_far,
    near_in, far_in, beside_in, behind_in,
    grad, att, cot_low, cot_high, att_low, att_high, cot_pad, att_pad, att_f,
    kc, vc, dkp, dvp, taps_sum, taps_in,
    load_sem, send_sem, recv_sem, halo_send, halo_recv, taps_send, taps_recv,
):
    frames, width = q_ref.shape
    chunks = width // LANES
    held = frames // BLOCK
    me = lax.axis_index("seq")
    odd_core = (me % 2) == 1
    odd_pair = ((me // 2) % 2) == 1
    mate = jnp.where(odd_core, me - 1, me + 1)
    across = jnp.where(odd_pair, me - 2, me + 2)
    up = (me + SPAN_DEV) % count
    down = (me + count - SPAN_DEV) % count
    after = (me + 1) % count
    before = (me + count - 1) % count
    has_up = me < count - SPAN_DEV
    has_down = me >= SPAN_DEV
    has_after = me < count - 1
    has_before = me > 0
    rounds = count.bit_length() - 1

    def partner(step):
        bit = 1 << step
        return jnp.where((me // bit) % 2 == 1, me - bit, me + bit)

    def columns(c):
        return pl.ds(pl.multiple_of(c * LANES, LANES), LANES)

    def loads(c):
        return (
            pltpu.make_async_copy(k_hbm.at[:, columns(c)], own.at[c, 0], load_sem.at[0, c]),
            pltpu.make_async_copy(v_hbm.at[:, columns(c)], own.at[c, 1], load_sem.at[1, c]),
        )

    def copy(kind, c, source, target_ref, device):
        return pltpu.make_async_remote_copy(
            src_ref=source.at[c], dst_ref=target_ref.at[c],
            send_sem=send_sem.at[kind, c], recv_sem=recv_sem.at[kind, c],
            device_id={"seq": device}, device_id_type=MESH,
        )

    def send_z(c):
        return copy(Z, c, own, behind, up)

    def send_y(c, source):
        return copy(Y, c, source, beside, across)

    def send_m(c, source):
        return copy(M, c, source, near, mate)

    def send_d(c):
        return copy(D, c, beside, far, mate)

    def return_m(c):
        return copy(BM, c, g_near, near_in, mate)

    def return_d(c):
        return copy(BD, c, g_far, far_in, mate)

    def return_y(c):
        return copy(BY, c, g_beside, beside_in, across)

    def return_z(c):
        return copy(BZ, c, g_behind, behind_in, down)

    def halo(index, source, target_ref, device):
        return pltpu.make_async_remote_copy(
            src_ref=source, dst_ref=target_ref,
            send_sem=halo_send.at[index], recv_sem=halo_recv.at[index],
            device_id={"seq": device}, device_id_type=MESH,
        )

    def halo_up(index, rows, target_ref):
        return halo(index, rows.at[pl.ds(frames - HALO, HALO)], target_ref, after)

    def halo_down(index, rows, target_ref):
        return halo(index, rows.at[pl.ds(0, HALO)], target_ref, before)

    def start_halo(index, rows, low, high):
        @pl.when(has_after)
        def _():
            halo_up(index, rows, low).start()

        @pl.when(has_before)
        def _():
            halo_down(index + 1, rows, high).start()

    def wait_halo(index, rows, low, high):
        @pl.when(has_before)
        def _():
            halo_up(index, rows, low).wait_recv()

        @pl.when(has_after)
        def _():
            halo_down(index + 1, rows, high).wait_recv()

    def drain_halo(index, rows, low, high):
        @pl.when(has_after)
        def _():
            halo_up(index, rows, low).wait_send()

        @pl.when(has_before)
        def _():
            halo_down(index + 1, rows, high).wait_send()

    def start_loads(c, carry):
        for load in loads(c):
            load.start()
        return carry

    lax.fori_loop(0, chunks, start_loads, 0)

    @pl.when(jnp.logical_not(has_before))
    def _():
        cot_low[...] = jnp.zeros_like(cot_low)
        att_low[...] = jnp.zeros_like(att_low)

    @pl.when(jnp.logical_not(has_after))
    def _():
        cot_high[...] = jnp.zeros_like(cot_high)
        att_high[...] = jnp.zeros_like(att_high)

    @pl.when(jnp.logical_not(has_down))
    def _():
        behind[...] = jnp.zeros_like(behind)

    @pl.when(jnp.logical_not(has_up))
    def _():
        behind_in[...] = jnp.zeros_like(behind_in)

    barrier = pltpu.get_barrier_semaphore()

    def greet(device):
        pl.semaphore_signal(barrier, inc=1, device_id={"seq": device}, device_id_type=MESH)

    for step in range(rounds):
        greet(partner(step))
    for flag, device in ((has_up, up), (has_down, down), (has_after, after), (has_before, before)):
        pl.when(flag)(functools.partial(greet, device))
    peers = jnp.int32(rounds)
    for flag in (has_up, has_down, has_after, has_before):
        peers = peers + jnp.where(flag, 1, 0)
    pl.semaphore_wait(barrier, peers)

    start_halo(0, cot_ref, cot_low, cot_high)

    def start_sends(c, carry):
        for load in loads(c):
            load.wait()

        @pl.when(has_up)
        def _():
            send_z(c).start()

        @pl.when(jnp.logical_not(odd_core))
        def _():
            send_m(c, own).start()

        @pl.when(jnp.logical_not(odd_pair))
        def _():
            send_y(c, own).start()

        return carry

    lax.fori_loop(0, chunks, start_sends, 0)
    wait_halo(0, cot_ref, cot_low, cot_high)

    def relay_first(c):
        @pl.when(has_down)
        def _():
            send_z(c).wait_recv()

        @pl.when(odd_pair)
        def _():
            send_y(c, behind).start()

        @pl.when(odd_core)
        def _():
            send_m(c, behind).start()

    def relay_second(c):
        send_y(c, own).wait_recv()
        send_d(c).start()

    def convolve(c, pad, at, out_ref, flip):
        for base in range(0, frames, ROWS):
            total = jnp.zeros((ROWS, LANES), jnp.float32)
            for tap in range(KERNEL):
                reach = HALF - tap if flip else tap - HALF
                start = base + HALO + reach
                total += taps_ref[tap:tap + 1, columns(c)] * pad[at, start:start + ROWS, :]
            out_ref[base:base + ROWS, columns(c)] = total.astype(out_ref.dtype)

    def fill(c, pad, at, low, rows, high):
        pad[at, 0:HALO] = low[:, columns(c)].astype(jnp.float32)
        pad[at, HALO:HALO + frames] = rows[:, columns(c)].astype(jnp.float32)
        pad[at, HALO + frames:2 * HALO + frames] = high[:, columns(c)].astype(jnp.float32)

    def backward_conv(c, carry):
        fill(c, cot_pad, c, cot_low, cot_ref, cot_high)
        convolve(c, cot_pad, c, grad, True)
        return carry

    third = chunks // 2
    lax.fori_loop(0, third, backward_conv, 0)
    for c in range(AHEAD):
        relay_first(c)
    lax.fori_loop(third, chunks, backward_conv, 0)
    for c in range(AHEAD, 2 * AHEAD):
        relay_first(c)
    for c in range(AHEAD):
        relay_second(c)

    dkp[LOOK * held] = jnp.zeros((BLOCK, LANES), jnp.float32)
    dvp[LOOK * held] = jnp.zeros((BLOCK, LANES), jnp.float32)

    def attend(c):
        low_head = lax.broadcasted_iota(jnp.int32, (BLOCK, LANES), 1) < HD

        def both(rows):
            zero = jnp.zeros_like(rows)
            return jnp.concatenate(
                [jnp.where(low_head, rows, zero), jnp.where(low_head, zero, rows)], axis=0
            )

        shape = (held, BLOCK, LANES)
        for place, ref in enumerate((own, behind, near, beside, far)):
            at = held * place
            kc[at:at + held] = ref[c, 0].reshape(shape)
            vc[at:at + held] = ref[c, 1].reshape(shape)
        for block in range(held):
            rows = slice(block * BLOCK, (block + 1) * BLOCK)
            query = both(q_ref[rows, columns(c)] * SCALE)
            gradient = both(grad[rows, columns(c)])
            spots = [slots[block, j] for j in range(LOOK)]
            kk = jnp.concatenate([kc[s] for s in spots], axis=0)
            vv = jnp.concatenate([vc[s] for s in spots], axis=0)
            scores = dot(kk, query, NT)
            scores = jnp.concatenate(
                [scores[j * BLOCK:(j + 1) * BLOCK] + bias[block, j] for j in range(LOOK)], axis=0
            )
            peak = jnp.max(scores, axis=0, keepdims=True)
            expo = jnp.exp(scores - peak)
            probs = expo * (1.0 / jnp.sum(expo, axis=0, keepdims=True))
            probs_half = probs.astype(jnp.bfloat16)
            out = dot(probs_half, vv, TN)
            att[rows, columns(c)] = jnp.where(low_head, out[:BLOCK], out[BLOCK:]).astype(att.dtype)
            probs_grad = dot(vv, gradient, NT)
            delta = jnp.sum(probs_half.astype(jnp.float32) * probs_grad, axis=0, keepdims=True)
            scores_grad = (probs * (probs_grad - delta)).astype(jnp.bfloat16)
            turned = dot(scores_grad, kk, TN)
            dq_ref[rows, columns(c)] = (
                SCALE * jnp.where(low_head, turned[:BLOCK], turned[BLOCK:])
            ).astype(dq_ref.dtype)
            some = slice(block * LOOK, (block + 1) * LOOK)
            dkp[some] = dot(scores_grad, query, NN).reshape(LOOK, BLOCK, LANES)
            dvp[some] = dot(probs_half, gradient, NN).reshape(LOOK, BLOCK, LANES)
        for place, ref in enumerate((g_own, g_behind, g_near, g_beside, g_far)):
            for half in range(held):
                rows = slice(half * BLOCK, (half + 1) * BLOCK)
                picks = [back[place * held + half, block] for block in range(held)]
                ref[c, 0, rows] = sum(dkp[p] for p in picks).astype(ref.dtype)
                ref[c, 1, rows] = sum(dvp[p] for p in picks).astype(ref.dtype)

    def wide(ref, c):
        return ref[c].astype(jnp.float32)

    def return_second(c):
        return_d(c).wait_recv()
        g_beside[c] = (wide(g_beside, c) + wide(far_in, c)).astype(jnp.bfloat16)
        return_y(c).start()

    def return_third(c):
        return_m(c).wait_recv()
        return_y(c).wait_recv()
        one, two = wide(near_in, c), wide(beside_in, c)
        g_own[c] = (
            wide(g_own, c) + jnp.where(odd_core, 0.0, one) + jnp.where(odd_pair, 0.0, two)
        ).astype(jnp.bfloat16)
        g_behind[c] = (
            wide(g_behind, c) + jnp.where(odd_core, one, 0.0) + jnp.where(odd_pair, two, 0.0)
        ).astype(jnp.bfloat16)

        @pl.when(has_down)
        def _():
            return_z(c).start()

    def return_last(c, carry):
        @pl.when(has_up)
        def _():
            return_z(c).wait_recv()

        total = (wide(g_own, c) + wide(behind_in, c)).astype(jnp.bfloat16)
        dk_ref[:, columns(c)] = total[0]
        dv_ref[:, columns(c)] = total[1]
        return carry

    def step(c, carry):
        pl.when(c + 2 * AHEAD < chunks)(lambda: relay_first(c + 2 * AHEAD))
        pl.when(c + AHEAD < chunks)(lambda: relay_second(c + AHEAD))
        send_m(c, own).wait_recv()
        send_d(c).wait_recv()
        attend(c)
        return_m(c).start()
        return_d(c).start()
        pl.when(c >= 1)(lambda: return_second(c - 1))
        pl.when(c >= 3)(lambda: return_third(c - 3))
        return carry

    lax.fori_loop(0, chunks, step, 0)
    start_halo(2, att, att_low, att_high)

    def taps_gradient(c, carry):
        att_f[...] = att[:, columns(c)].astype(jnp.float32)
        for tap in range(KERNEL):
            start = HALO + HALF - tap
            taps_sum[tap:tap + 1, columns(c)] = jnp.sum(
                att_f[...] * cot_pad[c, start:start + frames, :], axis=0, keepdims=True
            )
        return carry

    taps_sum[KERNEL:TAPS] = jnp.zeros((TAPS - KERNEL, width), jnp.float32)
    cut = chunks // 3
    lax.fori_loop(0, cut, taps_gradient, 0)
    return_second(chunks - 1)
    return_third(chunks - 3)
    lax.fori_loop(cut, 2 * cut, taps_gradient, 0)
    return_third(chunks - 2)
    lax.fori_loop(2 * cut, chunks, taps_gradient, 0)
    return_third(chunks - 1)
    wait_halo(2, att, att_low, att_high)

    def forward_conv(c, carry):
        fill(c, att_pad, 0, att_low, att, att_high)
        convolve(c, att_pad, 0, conv_ref, False)
        return carry

    edges = [r * chunks // rounds for r in range(rounds + 1)]
    for r in range(rounds):
        exchange = pltpu.make_async_remote_copy(
            src_ref=taps_sum, dst_ref=taps_in.at[r],
            send_sem=taps_send.at[r], recv_sem=taps_recv.at[r],
            device_id={"seq": partner(r)}, device_id_type=MESH,
        )
        exchange.start()
        lax.fori_loop(edges[r], edges[r + 1], forward_conv, 0)
        exchange.wait()
        taps_sum[...] += taps_in[r]
    kg_ref[...] = taps_sum[0:KERNEL]
    lax.fori_loop(0, chunks, return_last, 0)

    def drain(c, carry):
        pl.when(has_up)(lambda: send_z(c).wait_send())
        send_y(c, own).wait_send()
        send_m(c, own).wait_send()
        send_d(c).wait_send()
        return_m(c).wait_send()
        return_d(c).wait_send()
        return_y(c).wait_send()
        pl.when(has_down)(lambda: return_z(c).wait_send())
        return carry

    lax.fori_loop(0, chunks, drain, 0)
    drain_halo(0, cot_ref, cot_low, cot_high)
    drain_halo(2, att, att_low, att_high)


def local(query, keys, values, allowed, kernel, cotangent):
    frames, width = query.shape
    held = frames // BLOCK
    count = lax.axis_size("seq")
    me = lax.axis_index("seq")
    chunks = width // LANES
    distance = jnp.clip(me - jnp.maximum(allowed, 0) // held, 0, SPAN_DEV)
    odd = (me % 2) == 1
    place = jnp.where(distance == 4, 1, jnp.where(distance == 2, 3, 0))
    place = jnp.where(distance == 1, jnp.where(odd, 2, 4), place)
    place = jnp.where(distance == 3, jnp.where(odd, 4, 2), place)
    valid = allowed >= 0
    slots = jnp.where(valid, place * held + allowed % held, 0).astype(jnp.int32)
    bias = jnp.where(valid, 0.0, NEG).astype(jnp.float32)
    spots = jnp.arange(held * (SPAN_DEV + 1), dtype=jnp.int32)
    hit = (slots[None] == spots[:, None, None]) & valid[None]
    order = jnp.arange(held * LOOK, dtype=jnp.int32).reshape(held, LOOK)
    back = jnp.min(jnp.where(hit, order[None], held * LOOK), axis=2).astype(jnp.int32)

    vmem = pl.BlockSpec(memory_space=pltpu.VMEM)
    smem = pl.BlockSpec(memory_space=pltpu.SMEM)
    hbm = pl.BlockSpec(memory_space=pl.ANY)
    half, full = jnp.bfloat16, jnp.float32
    pair = pltpu.VMEM((chunks, 2, frames, LANES), half)
    flat = pltpu.VMEM((frames, width), half)
    edge = pltpu.VMEM((HALO, width), half)
    padded = frames + 2 * HALO
    blocks = held * (SPAN_DEV + 1)
    parts = held * LOOK + 1
    rounds = count.bit_length() - 1
    out = jax.ShapeDtypeStruct((frames, width), half)
    dma = pltpu.SemaphoreType.DMA
    return pl.pallas_call(
        functools.partial(whole_kernel, count),
        in_specs=[smem, smem, smem, vmem, hbm, hbm, vmem, vmem],
        out_specs=[vmem] * 5,
        out_shape=[out, out, out, out, jax.ShapeDtypeStruct((KERNEL, width), full)],
        scratch_shapes=[pair] * 14 + [flat] * 2 + [edge] * 4 + [
            pltpu.VMEM((chunks, padded, LANES), full),
            pltpu.VMEM((1, padded, LANES), full),
            pltpu.VMEM((frames, LANES), full),
            pltpu.VMEM((blocks, BLOCK, LANES), half),
            pltpu.VMEM((blocks, BLOCK, LANES), half),
            pltpu.VMEM((parts, BLOCK, LANES), full),
            pltpu.VMEM((parts, BLOCK, LANES), full),
            pltpu.VMEM((TAPS, width), full),
            pltpu.VMEM((rounds, TAPS, width), full),
            dma((2, chunks)), dma((8, chunks)), dma((8, chunks)),
            dma((4,)), dma((4,)), dma((rounds,)), dma((rounds,)),
        ],
        compiler_params=pltpu.CompilerParams(
            collective_id=0, has_side_effects=True, vmem_limit_bytes=56 * 1024 * 1024
        ),
    )(slots, back, bias, query, keys, values, kernel, cotangent)


def solution(mesh):
    rows = P(("groups", "seq"), None)
    return jax.shard_map(
        local,
        mesh=mesh,
        in_specs=(rows, rows, rows, rows, P(), rows),
        out_specs=(rows, rows, rows, rows, P("groups", None)),
        check_vma=False,
    )
```

```python
import functools

import jax
import jax.numpy as jnp
from jax import lax
from jax.experimental import pallas as pl
from jax.experimental.pallas import tpu as pltpu
from jax.sharding import PartitionSpec as P

HD = 64
KERNEL = 31
HALF = KERNEL // 2
TAPS = 32
BLOCK = 128
LOOK = 4
SPAN_DEV = 4
LANES = 128
HALO = 16
ROWS = 64
AHEAD = 2

SCALE = 0.125
NEG = -1e30
NT = (((1,), (1,)), ((), ()))
TN = (((0,), (0,)), ((), ()))
NN = (((1,), (0,)), ((), ()))
MESH = pl.DeviceIdType.MESH
Z, Y, M, D, BM, BD, BY, BZ = range(8)


def dot(a, b, dims):
    return lax.dot_general(a, b, dims, preferred_element_type=jnp.float32)


def whole_kernel(
    count, slots, back, bias, q_ref, k_hbm, v_hbm, taps_ref, cot_ref,
    conv_ref, dq_ref, dk_ref, dv_ref, kg_ref,
    own, behind, near, beside, far,
    g_own, g_behind, g_near, g_beside, g_far,
    near_in, far_in, beside_in, behind_in,
    grad, att, cot_low, cot_high, att_low, att_high, cot_pad, att_pad, att_f,
    kc, vc, dkp, dvp, taps_sum, taps_in, half_in, half_back, quarter_in, quarter_back,
    load_sem, send_sem, recv_sem, halo_send, halo_recv, taps_send, taps_recv,
):
    frames, width = q_ref.shape
    chunks = width // LANES
    held = frames // BLOCK
    me = lax.axis_index("seq")
    odd_core = (me % 2) == 1
    odd_pair = ((me // 2) % 2) == 1
    mate = jnp.where(odd_core, me - 1, me + 1)
    across = jnp.where(odd_pair, me - 2, me + 2)
    up = (me + SPAN_DEV) % count
    down = (me + count - SPAN_DEV) % count
    after = (me + 1) % count
    before = (me + count - 1) % count
    has_up = me < count - SPAN_DEV
    has_down = me >= SPAN_DEV
    has_after = me < count - 1
    has_before = me > 0
    rounds = count.bit_length() - 1

    def partner(step):
        bit = 1 << step
        return jnp.where((me // bit) % 2 == 1, me - bit, me + bit)

    def columns(c):
        return pl.ds(pl.multiple_of(c * LANES, LANES), LANES)

    def loads(c):
        return (
            pltpu.make_async_copy(k_hbm.at[:, columns(c)], own.at[c, 0], load_sem.at[0, c]),
            pltpu.make_async_copy(v_hbm.at[:, columns(c)], own.at[c, 1], load_sem.at[1, c]),
        )

    def copy(kind, c, source, target_ref, device):
        return pltpu.make_async_remote_copy(
            src_ref=source.at[c], dst_ref=target_ref.at[c],
            send_sem=send_sem.at[kind, c], recv_sem=recv_sem.at[kind, c],
            device_id={"seq": device}, device_id_type=MESH,
        )

    def send_z(c):
        return copy(Z, c, own, behind, up)

    def send_y(c, source):
        return copy(Y, c, source, beside, across)

    def send_m(c, source):
        return copy(M, c, source, near, mate)

    def send_d(c):
        return copy(D, c, beside, far, mate)

    def return_m(c):
        return copy(BM, c, g_near, near_in, mate)

    def return_d(c):
        return copy(BD, c, g_far, far_in, mate)

    def return_y(c):
        return copy(BY, c, g_beside, beside_in, across)

    def return_z(c):
        return copy(BZ, c, g_behind, behind_in, down)

    def halo(index, source, target_ref, device):
        return pltpu.make_async_remote_copy(
            src_ref=source, dst_ref=target_ref,
            send_sem=halo_send.at[index], recv_sem=halo_recv.at[index],
            device_id={"seq": device}, device_id_type=MESH,
        )

    def halo_up(index, rows, target_ref):
        return halo(index, rows.at[pl.ds(frames - HALO, HALO)], target_ref, after)

    def halo_down(index, rows, target_ref):
        return halo(index, rows.at[pl.ds(0, HALO)], target_ref, before)

    def start_halo(index, rows, low, high):
        @pl.when(has_after)
        def _():
            halo_up(index, rows, low).start()

        @pl.when(has_before)
        def _():
            halo_down(index + 1, rows, high).start()

    def wait_halo(index, rows, low, high):
        @pl.when(has_before)
        def _():
            halo_up(index, rows, low).wait_recv()

        @pl.when(has_after)
        def _():
            halo_down(index + 1, rows, high).wait_recv()

    def drain_halo(index, rows, low, high):
        @pl.when(has_after)
        def _():
            halo_up(index, rows, low).wait_send()

        @pl.when(has_before)
        def _():
            halo_down(index + 1, rows, high).wait_send()

    def start_loads(c, carry):
        for load in loads(c):
            load.start()
        return carry

    lax.fori_loop(0, chunks, start_loads, 0)

    @pl.when(jnp.logical_not(has_before))
    def _():
        cot_low[...] = jnp.zeros_like(cot_low)
        att_low[...] = jnp.zeros_like(att_low)

    @pl.when(jnp.logical_not(has_after))
    def _():
        cot_high[...] = jnp.zeros_like(cot_high)
        att_high[...] = jnp.zeros_like(att_high)

    @pl.when(jnp.logical_not(has_down))
    def _():
        behind[...] = jnp.zeros_like(behind)

    @pl.when(jnp.logical_not(has_up))
    def _():
        behind_in[...] = jnp.zeros_like(behind_in)

    barrier = pltpu.get_barrier_semaphore()

    def greet(device):
        pl.semaphore_signal(barrier, inc=1, device_id={"seq": device}, device_id_type=MESH)

    for step in range(rounds):
        greet(partner(step))
    for flag, device in ((has_up, up), (has_down, down), (has_after, after), (has_before, before)):
        pl.when(flag)(functools.partial(greet, device))
    peers = jnp.int32(rounds)
    for flag in (has_up, has_down, has_after, has_before):
        peers = peers + jnp.where(flag, 1, 0)
    pl.semaphore_wait(barrier, peers)

    start_halo(0, cot_ref, cot_low, cot_high)

    def start_sends(c, carry):
        for load in loads(c):
            load.wait()

        @pl.when(has_up)
        def _():
            send_z(c).start()

        @pl.when(jnp.logical_not(odd_core))
        def _():
            send_m(c, own).start()

        @pl.when(jnp.logical_not(odd_pair))
        def _():
            send_y(c, own).start()

        return carry

    lax.fori_loop(0, chunks, start_sends, 0)
    wait_halo(0, cot_ref, cot_low, cot_high)

    def relay_first(c):
        @pl.when(has_down)
        def _():
            send_z(c).wait_recv()

        @pl.when(odd_pair)
        def _():
            send_y(c, behind).start()

        @pl.when(odd_core)
        def _():
            send_m(c, behind).start()

    def relay_second(c):
        send_y(c, own).wait_recv()
        send_d(c).start()

    def convolve(c, pad, at, out_ref, flip):
        for base in range(0, frames, ROWS):
            total = jnp.zeros((ROWS, LANES), jnp.float32)
            for tap in range(KERNEL):
                reach = HALF - tap if flip else tap - HALF
                start = base + HALO + reach
                total += taps_ref[tap:tap + 1, columns(c)] * pad[at, start:start + ROWS, :]
            out_ref[base:base + ROWS, columns(c)] = total.astype(out_ref.dtype)

    def fill(c, pad, at, low, rows, high):
        pad[at, 0:HALO] = low[:, columns(c)].astype(jnp.float32)
        pad[at, HALO:HALO + frames] = rows[:, columns(c)].astype(jnp.float32)
        pad[at, HALO + frames:2 * HALO + frames] = high[:, columns(c)].astype(jnp.float32)

    def backward_conv(c, carry):
        fill(c, cot_pad, c, cot_low, cot_ref, cot_high)
        convolve(c, cot_pad, c, grad, True)
        return carry

    third = chunks // 2
    lax.fori_loop(0, third, backward_conv, 0)
    for c in range(AHEAD):
        relay_first(c)
    lax.fori_loop(third, chunks, backward_conv, 0)
    for c in range(AHEAD, 2 * AHEAD):
        relay_first(c)
    for c in range(AHEAD):
        relay_second(c)

    dkp[LOOK * held] = jnp.zeros((BLOCK, LANES), jnp.float32)
    dvp[LOOK * held] = jnp.zeros((BLOCK, LANES), jnp.float32)

    def attend(c):
        low_head = lax.broadcasted_iota(jnp.int32, (BLOCK, LANES), 1) < HD

        def both(rows):
            zero = jnp.zeros_like(rows)
            return jnp.concatenate(
                [jnp.where(low_head, rows, zero), jnp.where(low_head, zero, rows)], axis=0
            )

        def upright(sides):
            return jnp.concatenate([sides[:HD, :BLOCK], sides[HD:, BLOCK:]], axis=0).T

        shape = (held, BLOCK, LANES)
        for place, ref in enumerate((own, behind, near, beside, far)):
            at = held * place
            kc[at:at + held] = ref[c, 0].reshape(shape)
            vc[at:at + held] = ref[c, 1].reshape(shape)
        for block in range(held):
            rows = slice(block * BLOCK, (block + 1) * BLOCK)
            query = both(q_ref[rows, columns(c)] * SCALE)
            gradient = both(grad[rows, columns(c)])
            spots = [slots[block, j] for j in range(LOOK)]
            kk = jnp.concatenate([kc[s] for s in spots], axis=0)
            vv = jnp.concatenate([vc[s] for s in spots], axis=0)
            scores = dot(kk, query, NT)
            scores = jnp.concatenate(
                [scores[j * BLOCK:(j + 1) * BLOCK] + bias[block, j] for j in range(LOOK)], axis=0
            )
            peak = jnp.max(scores, axis=0, keepdims=True)
            expo = jnp.exp(scores - peak)
            probs = expo * (1.0 / jnp.sum(expo, axis=0, keepdims=True))
            probs_half = probs.astype(jnp.bfloat16)
            att[rows, columns(c)] = upright(dot(vv, probs_half, TN)).astype(att.dtype)
            probs_grad = dot(vv, gradient, NT)
            delta = jnp.sum(probs_half.astype(jnp.float32) * probs_grad, axis=0, keepdims=True)
            scores_grad = (probs * (probs_grad - delta)).astype(jnp.bfloat16)
            turned = upright(dot(kk, scores_grad, TN))
            dq_ref[rows, columns(c)] = (SCALE * turned).astype(dq_ref.dtype)
            some = slice(block * LOOK, (block + 1) * LOOK)
            dkp[some] = dot(scores_grad, query, NN).reshape(LOOK, BLOCK, LANES)
            dvp[some] = dot(probs_half, gradient, NN).reshape(LOOK, BLOCK, LANES)
        for place, ref in enumerate((g_own, g_behind, g_near, g_beside, g_far)):
            for half in range(held):
                rows = slice(half * BLOCK, (half + 1) * BLOCK)
                picks = [back[place * held + half, block] for block in range(held)]
                ref[c, 0, rows] = sum(dkp[p] for p in picks).astype(ref.dtype)
                ref[c, 1, rows] = sum(dvp[p] for p in picks).astype(ref.dtype)

    def wide(ref, c):
        return ref[c].astype(jnp.float32)

    def return_second(c):
        return_d(c).wait_recv()
        g_beside[c] = (wide(g_beside, c) + wide(far_in, c)).astype(jnp.bfloat16)
        return_y(c).start()

    def return_third(c):
        return_m(c).wait_recv()
        return_y(c).wait_recv()
        one, two = wide(near_in, c), wide(beside_in, c)
        g_own[c] = (
            wide(g_own, c) + jnp.where(odd_core, 0.0, one) + jnp.where(odd_pair, 0.0, two)
        ).astype(jnp.bfloat16)
        g_behind[c] = (
            wide(g_behind, c) + jnp.where(odd_core, one, 0.0) + jnp.where(odd_pair, two, 0.0)
        ).astype(jnp.bfloat16)

        @pl.when(has_down)
        def _():
            return_z(c).start()

    def return_last(c, carry):
        @pl.when(has_up)
        def _():
            return_z(c).wait_recv()

        total = (wide(g_own, c) + wide(behind_in, c)).astype(jnp.bfloat16)
        dk_ref[:, columns(c)] = total[0]
        dv_ref[:, columns(c)] = total[1]
        return carry

    def taps_gradient(c):
        att_f[...] = att[:, columns(c)].astype(jnp.float32)
        for tap in range(KERNEL):
            start = HALO + HALF - tap
            taps_sum[tap:tap + 1, columns(c)] = jnp.sum(
                att_f[...] * cot_pad[c, start:start + frames, :], axis=0, keepdims=True
            )

    taps_sum[KERNEL:TAPS] = jnp.zeros((TAPS - KERNEL, width), jnp.float32)

    def step(c, carry):
        pl.when(c + 2 * AHEAD < chunks)(lambda: relay_first(c + 2 * AHEAD))
        pl.when(c + AHEAD < chunks)(lambda: relay_second(c + AHEAD))
        send_m(c, own).wait_recv()
        send_d(c).wait_recv()
        attend(c)
        return_m(c).start()
        return_d(c).start()
        taps_gradient(c)
        pl.when(c >= 1)(lambda: return_second(c - 1))
        pl.when(c >= 3)(lambda: return_third(c - 3))
        return carry

    lax.fori_loop(0, chunks, step, 0)
    start_halo(2, att, att_low, att_high)

    def forward_conv(c, carry):
        fill(c, att_pad, 0, att_low, att, att_high)
        convolve(c, att_pad, 0, conv_ref, False)
        return carry

    def exchange(index, first, target_ref, device):
        size = target_ref.shape[-1]
        return pltpu.make_async_remote_copy(
            src_ref=taps_sum.at[:, pl.ds(pl.multiple_of(first, LANES), size)], dst_ref=target_ref,
            send_sem=taps_send.at[index], recv_sem=taps_recv.at[index],
            device_id={"seq": device}, device_id_type=MESH,
        )

    def span(first, size):
        return pl.ds(pl.multiple_of(first, LANES), size)

    most, quarter = width // 2, width // 4
    mine = jnp.where(odd_core, most, 0)
    other = most - mine
    kept = mine + jnp.where(odd_pair, quarter, 0)
    left = mine + jnp.where(odd_pair, 0, quarter)
    turns = rounds + 2
    edges = [r * chunks // turns for r in range(turns + 1)]

    def turn(index, first, target_ref, device):
        moving = exchange(index, first, target_ref, device)
        moving.start()
        return_pending(index)
        lax.fori_loop(edges[index], edges[index + 1], forward_conv, 0)
        moving.wait()

    def return_pending(index):
        if index == 0:
            return_second(chunks - 1)
            return_third(chunks - 3)
            return_third(chunks - 2)
            wait_halo(2, att, att_low, att_high)
        if index == 1:
            return_third(chunks - 1)

    turn(0, other, half_in, mate)
    taps_sum[:, span(mine, most)] += half_in[...]
    turn(1, left, quarter_in, across)
    taps_sum[:, span(kept, quarter)] += quarter_in[...]
    for r in range(2, rounds):
        turn(r, kept, taps_in.at[r - 2], partner(r))
        taps_sum[:, span(kept, quarter)] += taps_in[r - 2]
    turn(rounds, kept, quarter_back, across)
    taps_sum[:, span(left, quarter)] = quarter_back[...]
    turn(rounds + 1, mine, half_back, mate)
    taps_sum[:, span(other, most)] = half_back[...]
    kg_ref[...] = taps_sum[0:KERNEL]
    lax.fori_loop(0, chunks, return_last, 0)

    def drain(c, carry):
        pl.when(has_up)(lambda: send_z(c).wait_send())
        send_y(c, own).wait_send()
        send_m(c, own).wait_send()
        send_d(c).wait_send()
        return_m(c).wait_send()
        return_d(c).wait_send()
        return_y(c).wait_send()
        pl.when(has_down)(lambda: return_z(c).wait_send())
        return carry

    lax.fori_loop(0, chunks, drain, 0)
    drain_halo(0, cot_ref, cot_low, cot_high)
    drain_halo(2, att, att_low, att_high)


def local(query, keys, values, allowed, kernel, cotangent):
    frames, width = query.shape
    held = frames // BLOCK
    count = lax.axis_size("seq")
    me = lax.axis_index("seq")
    chunks = width // LANES
    distance = jnp.clip(me - jnp.maximum(allowed, 0) // held, 0, SPAN_DEV)
    odd = (me % 2) == 1
    place = jnp.where(distance == 4, 1, jnp.where(distance == 2, 3, 0))
    place = jnp.where(distance == 1, jnp.where(odd, 2, 4), place)
    place = jnp.where(distance == 3, jnp.where(odd, 4, 2), place)
    valid = allowed >= 0
    slots = jnp.where(valid, place * held + allowed % held, 0).astype(jnp.int32)
    bias = jnp.where(valid, 0.0, NEG).astype(jnp.float32)
    spots = jnp.arange(held * (SPAN_DEV + 1), dtype=jnp.int32)
    hit = (slots[None] == spots[:, None, None]) & valid[None]
    order = jnp.arange(held * LOOK, dtype=jnp.int32).reshape(held, LOOK)
    back = jnp.min(jnp.where(hit, order[None], held * LOOK), axis=2).astype(jnp.int32)

    vmem = pl.BlockSpec(memory_space=pltpu.VMEM)
    smem = pl.BlockSpec(memory_space=pltpu.SMEM)
    hbm = pl.BlockSpec(memory_space=pl.ANY)
    half, full = jnp.bfloat16, jnp.float32
    pair = pltpu.VMEM((chunks, 2, frames, LANES), half)
    flat = pltpu.VMEM((frames, width), half)
    edge = pltpu.VMEM((HALO, width), half)
    padded = frames + 2 * HALO
    blocks = held * (SPAN_DEV + 1)
    parts = held * LOOK + 1
    rounds = count.bit_length() - 1
    out = jax.ShapeDtypeStruct((frames, width), half)
    dma = pltpu.SemaphoreType.DMA
    return pl.pallas_call(
        functools.partial(whole_kernel, count),
        in_specs=[smem, smem, smem, vmem, hbm, hbm, vmem, vmem],
        out_specs=[vmem] * 5,
        out_shape=[out, out, out, out, jax.ShapeDtypeStruct((KERNEL, width), full)],
        scratch_shapes=[pair] * 14 + [flat] * 2 + [edge] * 4 + [
            pltpu.VMEM((chunks, padded, LANES), full),
            pltpu.VMEM((1, padded, LANES), full),
            pltpu.VMEM((frames, LANES), full),
            pltpu.VMEM((blocks, BLOCK, LANES), half),
            pltpu.VMEM((blocks, BLOCK, LANES), half),
            pltpu.VMEM((parts, BLOCK, LANES), full),
            pltpu.VMEM((parts, BLOCK, LANES), full),
            pltpu.VMEM((TAPS, width), full),
            pltpu.VMEM((rounds - 2, TAPS, width // 4), full),
            pltpu.VMEM((TAPS, width // 2), full),
            pltpu.VMEM((TAPS, width // 2), full),
            pltpu.VMEM((TAPS, width // 4), full),
            pltpu.VMEM((TAPS, width // 4), full),
            dma((2, chunks)), dma((8, chunks)), dma((8, chunks)),
            dma((4,)), dma((4,)), dma((rounds + 2,)), dma((rounds + 2,)),
        ],
        compiler_params=pltpu.CompilerParams(
            collective_id=0, has_side_effects=True, vmem_limit_bytes=56 * 1024 * 1024
        ),
    )(slots, back, bias, query, keys, values, kernel, cotangent)


def solution(mesh):
    rows = P(("groups", "seq"), None)
    return jax.shard_map(
        local,
        mesh=mesh,
        in_specs=(rows, rows, rows, rows, P(), rows),
        out_specs=(rows, rows, rows, rows, P("groups", None)),
        check_vma=False,
    )
```
